32 devices in a mesh: dp: 4 (over y, x), state: 8 (over z, core).
Axes of the slice: x: 2, y: 2, z: 4, core: 2. Of those that a mesh axis runs over, the one named last changes fastest.
Arguments:
- alpha_init: bfloat16 [32, 1024, 1024], P('dp', 'state'), may hold values from 0.099609375 to 4
- tokens: int32 [32, 3], P('dp'), may hold values from 0 to 511
- trans_rows: bfloat16 [1024, 1024], replicated, may hold values from 5e-05 to 1.11, as said below
- trans_cols: bfloat16 [1024, 1024], replicated, may hold values from 5e-05 to 1.11, as said below
- emit_rows: bfloat16 [512, 1024], replicated, may hold values from 0.001 to 1, as said below
- emit_cols: bfloat16 [512, 1024], replicated, may hold values from 0.001 to 1, as said below
- backward: bfloat16 [3, 32, 1024, 1024], P(None, 'dp', None, 'state'), may hold values from 0.2 to 32, as said below
Outputs:
- alpha_final: bfloat16 [32, 1024, 1024], P('dp', 'state')
- counts_rows: float32 [1024, 1024], P(None, ('dp', 'state'))
- counts_cols: float32 [1024, 1024], P(None, ('dp', 'state'))
- loglik: float32 [32], P('dp')
The draws below stay inside these ranges and needn't reach their ends.
Inputs may be any that keep to these rules, and one draw needn't show every extreme that they name: `trans_rows`: positive transition weights. `trans_cols`: positive transition weights. `emit_rows`: positive emission weights. `emit_cols`: positive emission weights. Positive backward weights.
All inputs are finite; a program needn't handle non-finite values.
Results may differ from the reference program's by a relative error of at most 0.0046.
Values may be sent and summed in bfloat16 or wider, within the bound.
A program may use at most 128 MiB of HBM per device.

```python
import math
import jax
import jax.numpy as jnp

K1 = 1024
K2 = 1024
VOCAB = 512
STEPS = 3
SEQ = 32
N_STATE = 8


def build_factor(key, width, marker):
    base = jax.random.fold_in(key, marker)
    key_floor, key_main, key_side, key_mainval, key_sideval = jax.random.split(base, 5)
    logs = jax.random.uniform(key_floor, (width, width), jnp.float32, math.log(5e-05), math.log(0.003))
    floor_part = jnp.exp(logs)
    main_value = jax.random.uniform(key_mainval, (width, 1), jnp.float32, 0.4, 0.7)
    side_value = jax.random.uniform(key_sideval, (width, 1), jnp.float32, 0.1, 0.3)
    main_order = jax.random.permutation(key_main, width)
    side_order = jax.random.permutation(key_side, width)
    columns = jnp.arange(width, dtype=jnp.int32)
    main_onehot = (main_order.astype(jnp.int32)[:, None] == columns[None, :]).astype(jnp.float32)
    side_onehot = (side_order.astype(jnp.int32)[:, None] == columns[None, :]).astype(jnp.float32)
    return floor_part + main_value * main_onehot + side_value * side_onehot


def build_emission(key, width, marker):
    base = jax.random.fold_in(key, marker)
    key_low = jax.random.fold_in(base, 1)
    logs = jax.random.uniform(key_low, (VOCAB, width), jnp.float32, math.log(0.001), 0.0)
    values = jnp.exp(logs)
    return values


def draw_trans_rows(key, part):
    return build_factor(key, K1, 101).astype(jnp.bfloat16)


def draw_trans_cols(key, part):
    return build_factor(key, K2, 202).astype(jnp.bfloat16)


def draw_emit_rows(key, part):
    return build_emission(key, K1, 404).astype(jnp.bfloat16)


def draw_emit_cols(key, part):
    return build_emission(key, K2, 505).astype(jnp.bfloat16)


def draw_backward(key, part):
    base = jax.random.fold_in(key, 303)
    key_vals, key_pair = jax.random.split(base, 2)
    logs = jax.random.uniform(key_vals, (STEPS, SEQ, K1, K2), jnp.float32, math.log(0.2), math.log(2.0))
    values = jnp.exp(logs)
    pairing = jax.random.permutation(key_pair, N_STATE).astype(jnp.int32)
    row_block = jnp.arange(K1, dtype=jnp.int32) // (K1 // N_STATE)
    col_block = jnp.arange(K2, dtype=jnp.int32) // (K2 // N_STATE)
    paired = (pairing[col_block][None, :] == row_block[:, None]).astype(jnp.float32)
    boost = 1.0 + 15.0 * paired
    return (values * boost[None, None, :, :]).astype(jnp.bfloat16)


def plant(drawn, rng, smallest, largest):
    spot = [jax.random.randint(jax.random.fold_in(rng, axis), (), 0, length) for axis, length in enumerate(drawn.shape)]
    main_axis = drawn.shape.index(max(drawn.shape))
    neighbour = spot[:main_axis] + [(spot[main_axis] + 1) % drawn.shape[main_axis]] + spot[main_axis + 1:]
    return drawn.at[tuple(spot)].set(smallest).at[tuple(neighbour)].set(largest)


def levels(own_key, shape, cuts, smallest, largest):
    gain, own = 1.0, jax.random.fold_in(own_key, 6)
    for position, parts in cuts:
        draws = jnp.exp(jax.random.uniform(jax.random.fold_in(own, position), (parts,), jnp.float32, smallest / len(cuts), largest / len(cuts)))
        gain = gain * jnp.repeat(draws, shape[position] // parts).reshape([-1 if axis == position else 1 for axis in range(len(shape))])
    return gain


def setup_inputs(seed: int = 0) -> dict:
    seeds = jax.random.split(jax.random.key(seed), 8)
    alpha_init = jnp.clip(jnp.exp(math.log(4.0) - 3.6927934 * jax.random.uniform(seeds[0], (SEQ, K1, K2), jnp.float32) ** levels(seeds[0], (SEQ, K1, K2), ((0, 4), (1, 8)), -0.2, 0.2)), 0.099609375, 4.0).astype(jnp.bfloat16)
    tokens = plant(jax.random.randint(seeds[1], (SEQ, STEPS), 0, VOCAB), jax.random.fold_in(seeds[1], 1), 0, VOCAB - 1).astype(jnp.int32)
    trans_rows = draw_trans_rows(jax.random.fold_in(seeds[7], 71), 0)
    trans_cols = draw_trans_cols(jax.random.fold_in(seeds[7], 71), 0)
    emit_rows = draw_emit_rows(jax.random.fold_in(seeds[7], 71), 0)
    emit_cols = draw_emit_cols(jax.random.fold_in(seeds[7], 71), 0)
    backward = draw_backward(jax.random.fold_in(seeds[7], 71), 0)
    return dict(alpha_init=alpha_init, tokens=tokens, trans_rows=trans_rows, trans_cols=trans_cols, emit_rows=emit_rows, emit_cols=emit_cols, backward=backward)


def reference(alpha_init, tokens, trans_rows, trans_cols, emit_rows, emit_cols, backward):
    f32 = jnp.float32
    alpha = alpha_init
    rows_f = trans_rows.astype(f32)
    cols_f = trans_cols.astype(f32)
    sums_rows = jnp.zeros((K1, K1), f32)
    sums_cols = jnp.zeros((K2, K2), f32)
    loglik = jnp.zeros((SEQ,), f32)
    for step in range(STEPS):
        tok = tokens[:, step]
        first = emit_rows[tok].astype(f32)
        second = emit_cols[tok].astype(f32)
        mixed = jnp.einsum("sij,jk->sik", alpha.astype(f32), cols_f).astype(jnp.bfloat16)
        moved = jnp.einsum("sik,il->slk", mixed.astype(f32), rows_f)
        emission = first[:, :, None] * second[:, None, :]
        scaled = moved * emission
        norm = jnp.sum(scaled, axis=(1, 2)) / (K1 * K2)
        weight = (emission * backward[step].astype(f32) / norm[:, None, None]).astype(jnp.bfloat16)
        pulled = jnp.einsum("il,slk->sik", rows_f, weight.astype(f32)).astype(jnp.bfloat16)
        sums_rows = sums_rows + jnp.einsum("sik,slk->il", mixed.astype(f32), weight.astype(f32))
        sums_cols = sums_cols + jnp.einsum("sij,sik->jk", alpha.astype(f32), pulled.astype(f32))
        loglik = loglik + jnp.log(norm)
        alpha = (scaled / norm[:, None, None]).astype(jnp.bfloat16)
    counts_rows = rows_f * sums_rows / (SEQ * STEPS)
    counts_cols = cols_f * sums_cols / (SEQ * STEPS)
    return (alpha, counts_rows, counts_cols, loglik)
```

```python
import functools

import jax
import jax.numpy as jnp
from jax import lax
from jax.experimental import pallas as pl
from jax.experimental.pallas import tpu as pltpu
from jax.sharding import PartitionSpec as P

STEPS = 3
F32 = jnp.float32
BF16 = jnp.bfloat16
NN = (((1,), (0,)), ((), ()))
NT = (((1,), (1,)), ((), ()))
TN = (((0,), (0,)), ((), ()))


def dot(a, b, dims=NN):
    return lax.dot_general(a, b, dims, preferred_element_type=F32)


def sequence_kernel(
    first_call,
    alpha_ref,
    rows_ref,
    rows_t_ref,
    cols_ref,
    rows_own_ref,
    cols_own_ref,
    back_mine_ref,
    back_other_ref,
    emit_l_ref,
    emit_k_ref,
    emit_l_own_ref,
    emit_k_own_ref,
    sum_l_ref,
    sum_k_ref,
    *rest,
):
    if first_call:
        final_ref, counts_r_ref, counts_c_ref, norm_ref = rest[:4]
    else:
        prev_r_ref, prev_c_ref, final_ref, counts_r_ref, counts_c_ref, norm_ref = rest[:6]
    ping, pong, mixed, mixed_own, weight, pulled = rest[-6:]
    width = alpha_ref.shape[0]
    cells = width * cols_ref.shape[1]
    half = back_mine_ref.shape[-1]
    tile = 256
    tiles = width // tile
    messages = (alpha_ref, ping, pong)
    for step in range(STEPS):
        alpha = messages[step]
        last = step == STEPS - 1
        v_row = sum_k_ref[step : step + 1, :]

        def mix(i, total, alpha=alpha, last=last, step=step, v_row=v_row):
            at = pl.ds(pl.multiple_of(i * tile, tile), tile)
            block = alpha[at, :]
            mixed_own[at, :] = dot(block, cols_own_ref[...]).astype(BF16)
            if not last:
                mixed[at, :] = dot(block, cols_ref[...]).astype(BF16)
            part = jnp.sum(block.astype(F32) * v_row, axis=1, keepdims=True)
            return total + jnp.sum(part * sum_l_ref[at, step : step + 1], axis=0, keepdims=True)

        total = lax.fori_loop(0, tiles, mix, jnp.zeros((1, 1), F32))
        norm = total / cells
        inv = 1.0 / norm
        norm_ref[step : step + 1, :] = jnp.broadcast_to(norm, (1, norm_ref.shape[1]))
        scaled_k = emit_k_own_ref[step : step + 1, :] * inv

        def weigh(i, carry, step=step, scaled_k=scaled_k):
            at = pl.ds(pl.multiple_of(i * tile, tile), tile)
            gain = emit_l_ref[at, step : step + 1]
            weight[at, :half] = (
                back_mine_ref[step, 0, at, :].astype(F32) * (gain * scaled_k[:, :half])
            ).astype(BF16)
            weight[at, half:] = (
                back_other_ref[step, 0, at, :].astype(F32) * (gain * scaled_k[:, half:])
            ).astype(BF16)
            return carry

        lax.fori_loop(0, tiles, weigh, 0)

        if not last:
            fresh = messages[step + 1]
            row_k = emit_k_ref[step : step + 1, :] * inv

            def move(i, carry, fresh=fresh, row_k=row_k, step=step):
                at = pl.ds(pl.multiple_of(i * tile, tile), tile)
                moved = dot(rows_t_ref[at, :], mixed[...])
                fresh[at, :] = (moved * (emit_l_ref[at, step : step + 1] * row_k)).astype(BF16)
                return carry

            lax.fori_loop(0, tiles, move, 0)
        else:
            held = dot(rows_own_ref[...], alpha[...]).astype(BF16)
            moved = dot(held, cols_ref[...])
            row_k = emit_k_ref[step : step + 1, :] * inv
            final_ref[...] = (moved * (emit_l_own_ref[:, step : step + 1] * row_k)).astype(BF16)

        def count(i, carry, step=step):
            at = pl.ds(pl.multiple_of(i * tile, tile), tile)
            pulled[at, :] = dot(rows_ref[at, :], weight[...]).astype(BF16)
            term = dot(weight[at, :], mixed_own[...], NT)
            if step > 0:
                counts_r_ref[at, :] += term
            elif first_call:
                counts_r_ref[at, :] = term
            else:
                counts_r_ref[at, :] = prev_r_ref[at, :] + term
            return carry

        lax.fori_loop(0, tiles, count, 0)
        term = dot(pulled[...], alpha[...], TN)
        if step > 0:
            counts_c_ref[...] += term
        elif first_call:
            counts_c_ref[...] = term
        else:
            counts_c_ref[...] = prev_c_ref[...] + term


def run_sequence(index, alpha, shared, back_mine, back_other, emits, previous):
    rows, rows_t, cols, rows_own, cols_own = shared
    width = alpha.shape[0]
    cols_all = cols.shape[1]
    own_rows = rows_own.shape[0]
    own_cols = cols_own.shape[1]
    half = back_mine.shape[-1]

    def whole(array):
        return pl.BlockSpec(array.shape, lambda i, n=array.ndim: (0,) * n)

    back_spec = pl.BlockSpec((STEPS, 1, width, half), lambda i: (0, index, 0, 0))
    operands = [alpha, rows, rows_t, cols, rows_own, cols_own, back_mine, back_other, *emits, *previous]
    specs = [whole(a) for a in operands]
    specs[6] = specs[7] = back_spec
    outs = [
        jax.ShapeDtypeStruct((own_rows, cols_all), BF16),
        jax.ShapeDtypeStruct((width, width), F32),
        jax.ShapeDtypeStruct((own_cols, cols_all), F32),
        jax.ShapeDtypeStruct((STEPS, 128), F32),
    ]
    flops = 2 * width * cols_all * (4 * width + 3 * 4 * own_cols + 2 * own_rows)
    return pl.pallas_call(
        functools.partial(sequence_kernel, not previous),
        grid=(1,),
        out_shape=outs,
        in_specs=[
            pl.BlockSpec(s.block_shape, s.index_map, pipeline_mode=pl.Buffered(1)) for s in specs
        ],
        out_specs=[whole(a) for a in outs],
        scratch_shapes=[
            pltpu.VMEM((width, cols_all), BF16),
            pltpu.VMEM((width, cols_all), BF16),
            pltpu.VMEM((width, cols_all), BF16),
            pltpu.VMEM((width, own_cols), BF16),
            pltpu.VMEM((width, own_cols), BF16),
            pltpu.VMEM((width, own_cols), BF16),
        ],
        compiler_params=pltpu.CompilerParams(vmem_limit_bytes=56 * 1024 * 1024),
        cost_estimate=pl.CostEstimate(flops=flops, bytes_accessed=24 * 1024 * 1024, transcendentals=0),
    )(*operands)


def on_device(alpha_init, tokens, trans_rows, trans_cols, emit_rows, emit_cols, backward):
    groups = lax.axis_size("state")
    dp = lax.axis_size("dp")
    me = lax.axis_index("state")
    core = me % 2
    seq_dev, rows_dev, width_cols = alpha_init.shape
    width_rows = trans_rows.shape[0]
    cols_dev = width_cols // groups
    half = seq_dev // 2
    pairs = [(d, d ^ 1) for d in range(groups)]
    lines = [list(range(c, groups, 2)) for c in range(2)]

    def swap(x):
        return lax.ppermute(x, "state", pairs)

    def split(x, axis):
        mine = lax.dynamic_slice_in_dim(x, core * half, half, axis)
        return mine, lax.dynamic_slice_in_dim(x, (1 - core) * half, half, axis)

    alpha_mine, alpha_send = split(alpha_init, 0)
    alpha_other = swap(alpha_send)
    chip_rows = jnp.where(
        core == 0,
        jnp.concatenate([alpha_mine, alpha_other], 1),
        jnp.concatenate([alpha_other, alpha_mine], 1),
    )
    back_mine, back_send = split(backward, 1)
    back_other = swap(back_send)

    def own(x, size, axis):
        return jnp.concatenate(
            [
                lax.dynamic_slice_in_dim(x, me * size, size, axis),
                lax.dynamic_slice_in_dim(x, (me + 1 - 2 * core) * size, size, axis),
            ],
            axis,
        )

    rows_t = trans_rows.T
    shared = (trans_rows, rows_t, trans_cols, own(rows_t, rows_dev, 0), own(trans_cols, cols_dev, 1))
    tok = lax.dynamic_slice_in_dim(tokens, core * half, half, 0)
    first = jnp.take(emit_rows, tok, axis=0)
    second = jnp.take(emit_cols, tok, axis=0)
    sum_l = jnp.einsum("stl,il->sit", first, trans_rows, preferred_element_type=F32)
    sum_k = jnp.einsum("stk,jk->stj", second, trans_cols, preferred_element_type=F32)
    emit_l = jnp.swapaxes(first, 1, 2).astype(F32)
    emit_k = second.astype(F32)
    emit_l_own = own(emit_l, rows_dev, 1)
    emit_k_own = own(emit_k, cols_dev, 2)

    previous = ()
    finals, norms = [], []
    for s in range(half):
        alpha = lax.all_gather(chip_rows[s], "state", axis=0, tiled=True, axis_index_groups=lines)
        emits = [x[s] for x in (emit_l, emit_k, emit_l_own, emit_k_own, sum_l, sum_k)]
        final, terms_r, terms_c, norm = run_sequence(
            s, alpha, shared, back_mine, back_other, emits, previous
        )
        previous = (terms_r, terms_c)
        finals.append(final)
        norms.append(norm[:, 0])

    final = jnp.stack(finals)
    final_mine, final_other = final[:, :rows_dev], swap(final[:, rows_dev:])
    alpha_final = jnp.where(
        core == 0,
        jnp.concatenate([final_mine, final_other], 0),
        jnp.concatenate([final_other, final_mine], 0),
    )
    logs = jnp.sum(jnp.log(jnp.stack(norms)), axis=1)
    logs_other = swap(logs)
    loglik = jnp.where(
        core == 0, jnp.concatenate([logs, logs_other]), jnp.concatenate([logs_other, logs])
    )

    factor = 1.0 / (seq_dev * dp * STEPS)
    block = width_rows // (groups * dp)
    place = lax.axis_index("dp") * groups + me
    sums_r = lax.psum_scatter(terms_r, ("dp", "state"), scatter_dimension=0, tiled=True)
    counts_rows = (
        lax.dynamic_slice_in_dim(rows_t, place * block, block, 0).astype(F32) * sums_r * factor
    ).T
    mine_c = terms_c[:cols_dev] + swap(terms_c[cols_dev:])
    sums_c = lax.psum_scatter(mine_c, "dp", scatter_dimension=0, tiled=True)
    order = [(d * groups + g, g * dp + d) for d in range(dp) for g in range(groups)]
    sums_c = lax.ppermute(sums_c, ("dp", "state"), order)
    col_block = width_cols // (groups * dp)
    counts_cols = (
        lax.dynamic_slice_in_dim(trans_cols, place * col_block, col_block, 1).astype(F32)
        * sums_c.T
        * factor
    )
    return (alpha_final, counts_rows, counts_cols, loglik)


def solution(mesh):
    return jax.shard_map(
        on_device,
        mesh=mesh,
        in_specs=(
            P("dp", "state", None),
            P("dp", None),
            P(),
            P(),
            P(),
            P(),
            P(None, "dp", None, "state"),
        ),
        out_specs=(
            P("dp", "state", None),
            P(None, ("dp", "state")),
            P(None, ("dp", "state")),
            P("dp"),
        ),
        check_vma=False,
    )
```

```python
import functools

import jax
import jax.numpy as jnp
from jax import lax
from jax.experimental import pallas as pl
from jax.experimental.pallas import tpu as pltpu
from jax.sharding import PartitionSpec as P

STEPS = 3
F32 = jnp.float32
BF16 = jnp.bfloat16
NN = (((1,), (0,)), ((), ()))
NT = (((1,), (1,)), ((), ()))
TN = (((0,), (0,)), ((), ()))


def dot(a, b, dims=NN):
    return lax.dot_general(a, b, dims, preferred_element_type=F32)


def sequence_kernel(
    first_call,
    alpha_ref,
    rows_ref,
    rows_t_ref,
    cols_ref,
    rows_own_ref,
    cols_own_ref,
    back_mine_ref,
    back_other_ref,
    emit_l_ref,
    emit_k_ref,
    emit_l_own_ref,
    emit_k_own_ref,
    sum_l_ref,
    sum_k_ref,
    *rest,
):
    if first_call:
        final_ref, counts_r_ref, counts_c_ref, norm_ref = rest[:4]
    else:
        prev_r_ref, prev_c_ref, final_ref, counts_r_ref, counts_c_ref, norm_ref = rest[:6]
    ping, pong, mixed, mixed_own, weight, pulled = rest[-6:]
    width = alpha_ref.shape[0]
    cells = width * cols_ref.shape[1]
    half = back_mine_ref.shape[-1]
    tile = 256
    tiles = width // tile
    messages = (alpha_ref, ping, pong)
    for step in range(STEPS):
        alpha = messages[step]
        last = step == STEPS - 1
        v_row = sum_k_ref[step : step + 1, :]

        def mix(i, total, alpha=alpha, last=last, step=step, v_row=v_row):
            at = pl.ds(pl.multiple_of(i * tile, tile), tile)
            block = alpha[at, :]
            mixed_own[at, :] = dot(block, cols_own_ref[...]).astype(BF16)
            if not last:
                mixed[at, :] = dot(block, cols_ref[...]).astype(BF16)
            part = jnp.sum(block.astype(F32) * v_row, axis=1, keepdims=True)
            return total + jnp.sum(part * sum_l_ref[at, step : step + 1], axis=0, keepdims=True)

        total = lax.fori_loop(0, tiles, mix, jnp.zeros((1, 1), F32))
        norm = total / cells
        inv = 1.0 / norm
        norm_ref[step : step + 1, :] = jnp.broadcast_to(norm, (1, norm_ref.shape[1]))
        scaled_k = emit_k_own_ref[step : step + 1, :] * inv

        def weigh(i, carry, step=step, scaled_k=scaled_k):
            at = pl.ds(pl.multiple_of(i * tile, tile), tile)
            gain = emit_l_ref[at, step : step + 1]
            weight[at, :half] = (
                back_mine_ref[step, 0, at, :].astype(F32) * (gain * scaled_k[:, :half])
            ).astype(BF16)
            weight[at, half:] = (
                back_other_ref[step, 0, at, :].astype(F32) * (gain * scaled_k[:, half:])
            ).astype(BF16)
            return carry

        lax.fori_loop(0, tiles, weigh, 0)

        if not last:
            fresh = messages[step + 1]
            row_k = emit_k_ref[step : step + 1, :] * inv

            def move(i, carry, fresh=fresh, row_k=row_k, step=step):
                at = pl.ds(pl.multiple_of(i * tile, tile), tile)
                moved = dot(rows_t_ref[at, :], mixed[...])
                fresh[at, :] = (moved * (emit_l_ref[at, step : step + 1] * row_k)).astype(BF16)
                return carry

            lax.fori_loop(0, tiles, move, 0)
        else:
            held = dot(rows_own_ref[...], alpha[...]).astype(BF16)
            moved = dot(held, cols_ref[...])
            row_k = emit_k_ref[step : step + 1, :] * inv
            final_ref[...] = (moved * (emit_l_own_ref[:, step : step + 1] * row_k)).astype(BF16)

        def count(i, carry, step=step):
            at = pl.ds(pl.multiple_of(i * tile, tile), tile)
            pulled[at, :] = dot(rows_ref[at, :], weight[...]).astype(BF16)
            term = dot(weight[at, :], mixed_own[...], NT)
            if step > 0:
                counts_r_ref[at, :] += term
            elif first_call:
                counts_r_ref[at, :] = term
            else:
                counts_r_ref[at, :] = prev_r_ref[at, :] + term
            return carry

        lax.fori_loop(0, tiles, count, 0)
        term = dot(pulled[...], alpha[...], TN)
        if step > 0:
            counts_c_ref[...] += term
        elif first_call:
            counts_c_ref[...] = term
        else:
            counts_c_ref[...] = prev_c_ref[...] + term


def run_sequence(index, alpha, shared, back_mine, back_other, emits, previous):
    rows, rows_t, cols, rows_own, cols_own = shared
    width = alpha.shape[0]
    cols_all = cols.shape[1]
    own_rows = rows_own.shape[0]
    own_cols = cols_own.shape[1]
    half = back_mine.shape[-1]

    def whole(array):
        return pl.BlockSpec(array.shape, lambda i, n=array.ndim: (0,) * n)

    back_spec = pl.BlockSpec((STEPS, 1, width, half), lambda i: (0, index, 0, 0))
    operands = [alpha, rows, rows_t, cols, rows_own, cols_own, back_mine, back_other, *emits, *previous]
    specs = [whole(a) for a in operands]
    specs[6] = specs[7] = back_spec
    outs = [
        jax.ShapeDtypeStruct((own_rows, cols_all), BF16),
        jax.ShapeDtypeStruct((width, width), F32),
        jax.ShapeDtypeStruct((own_cols, cols_all), F32),
        jax.ShapeDtypeStruct((STEPS, 128), F32),
    ]
    flops = 2 * width * cols_all * (4 * width + 3 * 4 * own_cols + 2 * own_rows)
    return pl.pallas_call(
        functools.partial(sequence_kernel, not previous),
        grid=(1,),
        out_shape=outs,
        in_specs=[
            pl.BlockSpec(s.block_shape, s.index_map, pipeline_mode=pl.Buffered(1)) for s in specs
        ],
        out_specs=[whole(a) for a in outs],
        scratch_shapes=[
            pltpu.VMEM((width, cols_all), BF16),
            pltpu.VMEM((width, cols_all), BF16),
            pltpu.VMEM((width, cols_all), BF16),
            pltpu.VMEM((width, own_cols), BF16),
            pltpu.VMEM((width, own_cols), BF16),
            pltpu.VMEM((width, own_cols), BF16),
        ],
        compiler_params=pltpu.CompilerParams(vmem_limit_bytes=56 * 1024 * 1024),
        cost_estimate=pl.CostEstimate(flops=flops, bytes_accessed=24 * 1024 * 1024, transcendentals=0),
    )(*operands)


def on_device(alpha_init, tokens, trans_rows, trans_cols, emit_rows, emit_cols, backward):
    groups = lax.axis_size("state")
    dp = lax.axis_size("dp")
    me = lax.axis_index("state")
    core = me % 2
    seq_dev, rows_dev, width_cols = alpha_init.shape
    width_rows = trans_rows.shape[0]
    cols_dev = width_cols // groups
    half = seq_dev // 2
    pairs = [(d, d ^ 1) for d in range(groups)]
    lines = [list(range(c, groups, 2)) for c in range(2)]

    def swap(x):
        return lax.ppermute(x, "state", pairs)

    def split(x, axis):
        mine = lax.dynamic_slice_in_dim(x, core * half, half, axis)
        return mine, lax.dynamic_slice_in_dim(x, (1 - core) * half, half, axis)

    alpha_mine, alpha_send = split(alpha_init, 0)
    alpha_other = swap(alpha_send)
    chip_rows = jnp.where(
        core == 0,
        jnp.concatenate([alpha_mine, alpha_other], 1),
        jnp.concatenate([alpha_other, alpha_mine], 1),
    )
    back_mine, back_send = split(backward, 1)
    back_other = swap(back_send)

    def own(x, size, axis):
        return jnp.concatenate(
            [
                lax.dynamic_slice_in_dim(x, me * size, size, axis),
                lax.dynamic_slice_in_dim(x, (me + 1 - 2 * core) * size, size, axis),
            ],
            axis,
        )

    rows_t = trans_rows.T
    shared = (trans_rows, rows_t, trans_cols, own(rows_t, rows_dev, 0), own(trans_cols, cols_dev, 1))
    tok = lax.dynamic_slice_in_dim(tokens, core * half, half, 0)
    first = jnp.take(emit_rows, tok, axis=0)
    second = jnp.take(emit_cols, tok, axis=0)
    sum_l = jnp.einsum("stl,il->sit", first, trans_rows, preferred_element_type=F32)
    sum_k = jnp.einsum("stk,jk->stj", second, trans_cols, preferred_element_type=F32)
    emit_l = jnp.swapaxes(first, 1, 2).astype(F32)
    emit_k = second.astype(F32)
    emit_l_own = own(emit_l, rows_dev, 1)
    emit_k_own = own(emit_k, cols_dev, 2)

    previous = ()
    finals, norms = [], []
    for s in range(half):
        alpha = lax.all_gather(chip_rows[s], "state", axis=0, tiled=True, axis_index_groups=lines)
        emits = [x[s] for x in (emit_l, emit_k, emit_l_own, emit_k_own, sum_l, sum_k)]
        final, terms_r, terms_c, norm = run_sequence(
            s, alpha, shared, back_mine, back_other, emits, previous
        )
        previous = (terms_r, terms_c)
        finals.append(final)
        norms.append(norm[:, 0])

    final = jnp.stack(finals)
    final_mine, final_other = final[:, :rows_dev], swap(final[:, rows_dev:])
    alpha_final = jnp.where(
        core == 0,
        jnp.concatenate([final_mine, final_other], 0),
        jnp.concatenate([final_other, final_mine], 0),
    )
    logs = jnp.sum(jnp.log(jnp.stack(norms)), axis=1)
    logs_other = swap(logs)
    loglik = jnp.where(
        core == 0, jnp.concatenate([logs, logs_other]), jnp.concatenate([logs_other, logs])
    )

    factor = 1.0 / (seq_dev * dp * STEPS)
    chips = groups // 2
    block = width_rows // (groups * dp)
    col_block = width_cols // (groups * dp)
    place = lax.axis_index("dp") * groups + me
    by_core = terms_r.reshape(dp, chips, 2, block, width_rows)

    def of_core(c, cols):
        rows = lax.dynamic_index_in_dim(by_core, c, 2, keepdims=False)
        return jnp.concatenate(
            [rows.reshape(dp, chips * block, width_rows), cols.reshape(dp, col_block, width_cols)], 1
        )

    here = of_core(core, terms_c[:cols_dev])
    there = swap(of_core(1 - core, terms_c[cols_dev:]).astype(BF16))
    both = (here + there.astype(F32)).astype(BF16)
    parts = lax.all_to_all(both, "dp", 0, 0, tiled=True)
    sums = jnp.sum(parts.astype(F32), axis=0)
    order = [(d * groups + g, g * dp + d) for d in range(dp) for g in range(groups)]
    sums_c = lax.ppermute(sums[chips * block :], ("dp", "state"), order)
    line = sums[: chips * block].reshape(chips, block, width_rows).astype(BF16)
    line = lax.all_to_all(line, "state", 0, 0, tiled=True, axis_index_groups=lines)
    sums_r = jnp.sum(line.astype(F32), axis=0)
    counts_rows = (
        lax.dynamic_slice_in_dim(rows_t, place * block, block, 0).astype(F32) * sums_r * factor
    ).T
    counts_cols = (
        lax.dynamic_slice_in_dim(trans_cols, place * col_block, col_block, 1).astype(F32)
        * sums_c.T
        * factor
    )
    return (alpha_final, counts_rows, counts_cols, loglik)


def solution(mesh):
    return jax.shard_map(
        on_device,
        mesh=mesh,
        in_specs=(
            P("dp", "state", None),
            P("dp", None),
            P(),
            P(),
            P(),
            P(),
            P(None, "dp", None, "state"),
        ),
        out_specs=(
            P("dp", "state", None),
            P(None, ("dp", "state")),
            P(None, ("dp", "state")),
            P("dp"),
        ),
        check_vma=False,
    )
```

```python
import functools

import jax
import jax.numpy as jnp
from jax import lax
from jax.experimental import pallas as pl
from jax.experimental.pallas import tpu as pltpu
from jax.sharding import PartitionSpec as P

STEPS = 3
F32 = jnp.float32
BF16 = jnp.bfloat16
NN = (((1,), (0,)), ((), ()))
NT = (((1,), (1,)), ((), ()))
TN = (((0,), (0,)), ((), ()))


def dot(a, b, dims=NN):
    return lax.dot_general(a, b, dims, preferred_element_type=F32)


def forward_kernel(
    chips,
    chip_ref,
    rows_ref,
    rows_t_ref,
    cols_ref,
    rows_own_ref,
    cols_own_ref,
    back_mine_ref,
    back_other_ref,
    emit_l_ref,
    emit_k_ref,
    emit_l_own_ref,
    emit_k_own_ref,
    sum_l_ref,
    sum_k_ref,
    final_ref,
    counts_r_ref,
    counts_c_ref,
    norm_ref,
    held,
    ping,
    pong,
    mixed,
    mixed_own,
    weight,
    pulled,
    send_sem,
    recv_sem,
):
    seqs, rows_chip, _ = chip_ref.shape
    width = rows_ref.shape[0]
    cells = width * cols_ref.shape[1]
    half = back_mine_ref.shape[-1]
    tile = 256
    tiles = width // tile
    hops = chips - 1
    me = lax.axis_index("state")
    core = lax.rem(me, 2)
    chip = me // 2
    right = lax.rem(chip + 1, chips) * 2 + core
    left = lax.rem(chip + chips - 1, chips) * 2 + core

    def rows_of(owner):
        return pl.ds(pl.multiple_of(owner * rows_chip, rows_chip), rows_chip)

    def hop(s, h):
        rows = rows_of(lax.rem(chip + chips - h, chips))
        return pltpu.make_async_remote_copy(
            src_ref=chip_ref.at[s] if h == 0 else held.at[s, rows],
            dst_ref=held.at[s, rows],
            send_sem=send_sem.at[s, h],
            recv_sem=recv_sem.at[s, h],
            device_id={"state": right},
            device_id_type=pl.DeviceIdType.MESH,
        )

    def advance(s, h):
        hop(s, h).wait_recv()
        if h + 1 < hops:
            hop(s, h + 1).start()

    barrier = pltpu.get_barrier_semaphore()
    for neighbour in (left, right):
        pl.semaphore_signal(
            barrier, inc=1, device_id={"state": neighbour}, device_id_type=pl.DeviceIdType.MESH
        )
    pl.semaphore_wait(barrier, 2)
    hop(0, 0).start()
    for s in range(seqs):
        held[s, rows_of(chip), :] = chip_ref[s]
    counts_r_ref[...] = jnp.zeros_like(counts_r_ref)
    counts_c_ref[...] = jnp.zeros_like(counts_c_ref)
    for h in range(hops):
        if h == hops - 1 and seqs > 1:
            hop(1, 0).start()
        advance(0, h)

    def sequence(s, carry):
        @pl.when(s + 2 < seqs)
        def _():
            hop(s + 2, 0).start()

        def follow(step):
            @pl.when(s + 1 < seqs)
            def _():
                for h in range(step * hops // STEPS, (step + 1) * hops // STEPS):
                    advance(s + 1, h)

        messages = (held.at[s], ping, pong)
        for step in range(STEPS):
            alpha = messages[step]
            last = step == STEPS - 1
            v_row = sum_k_ref[s, step : step + 1, :]

            def mix(i, total, alpha=alpha, last=last, step=step, v_row=v_row):
                at = pl.ds(pl.multiple_of(i * tile, tile), tile)
                block = alpha[at, :]
                mixed_own[at, :] = dot(block, cols_own_ref[...]).astype(BF16)
                if not last:
                    mixed[at, :] = dot(block, cols_ref[...]).astype(BF16)
                part = jnp.sum(block.astype(F32) * v_row, axis=1, keepdims=True)
                gain = sum_l_ref[s, at, step : step + 1]
                return total + jnp.sum(part * gain, axis=0, keepdims=True)

            total = lax.fori_loop(0, tiles, mix, jnp.zeros((1, 1), F32))
            norm = total / cells
            inv = 1.0 / norm
            norm_ref[s, step : step + 1, :] = jnp.broadcast_to(norm, (1, norm_ref.shape[2]))
            scaled_k = emit_k_own_ref[s, step : step + 1, :] * inv
            row_k = emit_k_ref[s, step : step + 1, :] * inv

            def weigh(i, carry, step=step, scaled_k=scaled_k):
                at = pl.ds(pl.multiple_of(i * tile, tile), tile)
                gain = emit_l_ref[s, at, step : step + 1]
                weight[at, :half] = (
                    back_mine_ref[step, s, at, :].astype(F32) * (gain * scaled_k[:, :half])
                ).astype(BF16)
                weight[at, half:] = (
                    back_other_ref[step, s, at, :].astype(F32) * (gain * scaled_k[:, half:])
                ).astype(BF16)
                return carry

            lax.fori_loop(0, tiles, weigh, 0)

            if not last:
                fresh = messages[step + 1]

                def move(i, carry, fresh=fresh, row_k=row_k, step=step):
                    at = pl.ds(pl.multiple_of(i * tile, tile), tile)
                    moved = dot(rows_t_ref[at, :], mixed[...])
                    gain = emit_l_ref[s, at, step : step + 1]
                    fresh[at, :] = (moved * (gain * row_k)).astype(BF16)
                    return carry

                lax.fori_loop(0, tiles, move, 0)
            else:
                rows_q = dot(rows_own_ref[...], alpha[...]).astype(BF16)
                moved = dot(rows_q, cols_ref[...])
                gain = emit_l_own_ref[s, :, step : step + 1]
                final_ref[s] = (moved * (gain * row_k)).astype(BF16)

            if not last:
                follow(step)

            def count(i, carry):
                at = pl.ds(pl.multiple_of(i * tile, tile), tile)
                pulled[at, :] = dot(rows_ref[at, :], weight[...]).astype(BF16)
                counts_r_ref[at, :] += dot(weight[at, :], mixed_own[...], NT)
                return carry

            lax.fori_loop(0, tiles, count, 0)
            counts_c_ref[...] += dot(pulled[...], alpha[...], TN)

            if last:
                follow(step)

        return carry

    lax.fori_loop(0, seqs, sequence, 0)
    for s in range(seqs):
        for h in range(hops):
            hop(s, h).wait_send()


def run_forward(chips, *operands):
    chip_rows, rows, _, cols, rows_own, cols_own = operands[:6]
    seqs = chip_rows.shape[0]
    width, cols_all = rows.shape[0], cols.shape[1]
    own_rows, own_cols = rows_own.shape[0], cols_own.shape[1]
    vmem = pl.BlockSpec(memory_space=pltpu.VMEM)
    flops = 2 * seqs * width * cols_all * (4 * width + 3 * 4 * own_cols + 2 * own_rows)
    message = pltpu.VMEM((width, cols_all), BF16)
    narrow = pltpu.VMEM((width, own_cols), BF16)
    return pl.pallas_call(
        functools.partial(forward_kernel, chips),
        out_shape=[
            jax.ShapeDtypeStruct((seqs, own_rows, cols_all), BF16),
            jax.ShapeDtypeStruct((width, width), F32),
            jax.ShapeDtypeStruct((own_cols, cols_all), F32),
            jax.ShapeDtypeStruct((seqs, STEPS, 128), F32),
        ],
        in_specs=[vmem] * len(operands),
        out_specs=[vmem] * 4,
        scratch_shapes=[
            pltpu.VMEM((seqs, width, cols_all), BF16),
            message,
            message,
            message,
            narrow,
            narrow,
            narrow,
            pltpu.SemaphoreType.DMA((seqs, chips - 1)),
            pltpu.SemaphoreType.DMA((seqs, chips - 1)),
        ],
        compiler_params=pltpu.CompilerParams(
            collective_id=0, has_side_effects=True, vmem_limit_bytes=58 * 1024 * 1024
        ),
        cost_estimate=pl.CostEstimate(
            flops=flops, bytes_accessed=40 * 1024 * 1024, transcendentals=0
        ),
    )(*operands)


def on_device(alpha_init, tokens, trans_rows, trans_cols, emit_rows, emit_cols, backward):
    groups = lax.axis_size("state")
    dp = lax.axis_size("dp")
    me = lax.axis_index("state")
    core = me % 2
    seq_dev, rows_dev, width_cols = alpha_init.shape
    width_rows = trans_rows.shape[0]
    cols_dev = width_cols // groups
    half = seq_dev // 2
    pairs = [(d, d ^ 1) for d in range(groups)]
    lines = [list(range(c, groups, 2)) for c in range(2)]

    def swap(x):
        return lax.ppermute(x, "state", pairs)

    def split(x, axis):
        mine = lax.dynamic_slice_in_dim(x, core * half, half, axis)
        return mine, lax.dynamic_slice_in_dim(x, (1 - core) * half, half, axis)

    alpha_mine, alpha_send = split(alpha_init, 0)
    alpha_other = swap(alpha_send)
    chip_rows = jnp.where(
        core == 0,
        jnp.concatenate([alpha_mine, alpha_other], 1),
        jnp.concatenate([alpha_other, alpha_mine], 1),
    )
    back_mine, back_send = split(backward, 1)
    back_other = swap(back_send)

    def own(x, size, axis):
        return jnp.concatenate(
            [
                lax.dynamic_slice_in_dim(x, me * size, size, axis),
                lax.dynamic_slice_in_dim(x, (me + 1 - 2 * core) * size, size, axis),
            ],
            axis,
        )

    rows_t = trans_rows.T
    shared = (trans_rows, rows_t, trans_cols, own(rows_t, rows_dev, 0), own(trans_cols, cols_dev, 1))
    tok = lax.dynamic_slice_in_dim(tokens, core * half, half, 0)
    first = jnp.take(emit_rows, tok, axis=0)
    second = jnp.take(emit_cols, tok, axis=0)
    sum_l = jnp.einsum("stl,il->sit", first, trans_rows, preferred_element_type=F32)
    sum_k = jnp.einsum("stk,jk->stj", second, trans_cols, preferred_element_type=F32)
    emit_l = jnp.swapaxes(first, 1, 2).astype(F32)
    emit_k = second.astype(F32)
    emit_l_own = own(emit_l, rows_dev, 1)
    emit_k_own = own(emit_k, cols_dev, 2)

    final, terms_r, terms_c, norms = run_forward(
        groups // 2,
        chip_rows,
        *shared,
        back_mine,
        back_other,
        emit_l,
        emit_k,
        emit_l_own,
        emit_k_own,
        sum_l,
        sum_k,
    )
    final_mine, final_other = final[:, :rows_dev], swap(final[:, rows_dev:])
    alpha_final = jnp.where(
        core == 0,
        jnp.concatenate([final_mine, final_other], 0),
        jnp.concatenate([final_other, final_mine], 0),
    )
    logs = jnp.sum(jnp.log(norms[:, :, 0]), axis=1)
    logs_other = swap(logs)
    loglik = jnp.where(
        core == 0, jnp.concatenate([logs, logs_other]), jnp.concatenate([logs_other, logs])
    )

    factor = 1.0 / (seq_dev * dp * STEPS)
    chips = groups // 2
    block = width_rows // (groups * dp)
    col_block = width_cols // (groups * dp)
    place = lax.axis_index("dp") * groups + me
    by_core = terms_r.reshape(dp, chips, 2, block, width_rows)

    def of_core(c, cols):
        rows = lax.dynamic_index_in_dim(by_core, c, 2, keepdims=False)
        return jnp.concatenate(
            [rows.reshape(dp, chips * block, width_rows), cols.reshape(dp, col_block, width_cols)], 1
        )

    here = of_core(core, terms_c[:cols_dev])
    there = swap(of_core(1 - core, terms_c[cols_dev:]).astype(BF16))
    both = (here + there.astype(F32)).astype(BF16)
    parts = lax.all_to_all(both, "dp", 0, 0, tiled=True)
    sums = jnp.sum(parts.astype(F32), axis=0)
    order = [(d * groups + g, g * dp + d) for d in range(dp) for g in range(groups)]
    sums_c = lax.ppermute(sums[chips * block :], ("dp", "state"), order)
    line = sums[: chips * block].reshape(chips, block, width_rows).astype(BF16)
    line = lax.all_to_all(line, "state", 0, 0, tiled=True, axis_index_groups=lines)
    sums_r = jnp.sum(line.astype(F32), axis=0)
    counts_rows = (
        lax.dynamic_slice_in_dim(rows_t, place * block, block, 0).astype(F32) * sums_r * factor
    ).T
    counts_cols = (
        lax.dynamic_slice_in_dim(trans_cols, place * col_block, col_block, 1).astype(F32)
        * sums_c.T
        * factor
    )
    return (alpha_final, counts_rows, counts_cols, loglik)


def solution(mesh):
    return jax.shard_map(
        on_device,
        mesh=mesh,
        in_specs=(
            P("dp", "state", None),
            P("dp", None),
            P(),
            P(),
            P(),
            P(),
            P(None, "dp", None, "state"),
        ),
        out_specs=(
            P("dp", "state", None),
            P(None, ("dp", "state")),
            P(None, ("dp", "state")),
            P("dp"),
        ),
        check_vma=False,
    )
```

```python
import functools

import jax
import jax.numpy as jnp
from jax import lax
from jax.experimental import pallas as pl
from jax.experimental.pallas import tpu as pltpu
from jax.sharding import PartitionSpec as P

STEPS = 3
F32 = jnp.float32
BF16 = jnp.bfloat16
NN = (((1,), (0,)), ((), ()))
NT = (((1,), (1,)), ((), ()))
TN = (((0,), (0,)), ((), ()))


def dot(a, b, dims=NN):
    return lax.dot_general(a, b, dims, preferred_element_type=F32)


def forward_kernel(
    chips,
    chip_ref,
    rows_ref,
    rows_t_ref,
    cols_ref,
    rows_own_ref,
    cols_own_ref,
    back_mine_ref,
    back_other_ref,
    emit_l_ref,
    emit_k_ref,
    emit_l_own_ref,
    emit_k_own_ref,
    sum_l_ref,
    sum_k_ref,
    final_ref,
    counts_r_ref,
    counts_c_ref,
    norm_ref,
    held,
    ping,
    pong,
    mixed,
    mixed_own,
    weight,
    pulled,
    send_sem,
    recv_sem,
):
    seqs, rows_chip, _ = chip_ref.shape
    width = rows_ref.shape[0]
    cells = width * cols_ref.shape[1]
    half = back_mine_ref.shape[-1]
    tile = 512
    tiles = width // tile
    hops = chips - 1
    me = lax.axis_index("state")
    core = lax.rem(me, 2)
    chip = me // 2
    right = lax.rem(chip + 1, chips) * 2 + core
    left = lax.rem(chip + chips - 1, chips) * 2 + core

    def rows_of(owner):
        return pl.ds(pl.multiple_of(owner * rows_chip, rows_chip), rows_chip)

    def hop(s, h):
        rows = rows_of(lax.rem(chip + chips - h, chips))
        return pltpu.make_async_remote_copy(
            src_ref=chip_ref.at[s] if h == 0 else held.at[s, rows],
            dst_ref=held.at[s, rows],
            send_sem=send_sem.at[s, h],
            recv_sem=recv_sem.at[s, h],
            device_id={"state": right},
            device_id_type=pl.DeviceIdType.MESH,
        )

    def advance(s, h):
        hop(s, h).wait_recv()
        if h + 1 < hops:
            hop(s, h + 1).start()

    barrier = pltpu.get_barrier_semaphore()
    for neighbour in (left, right):
        pl.semaphore_signal(
            barrier, inc=1, device_id={"state": neighbour}, device_id_type=pl.DeviceIdType.MESH
        )
    pl.semaphore_wait(barrier, 2)
    hop(0, 0).start()
    for s in range(seqs):
        held[s, rows_of(chip), :] = chip_ref[s]
    counts_r_ref[...] = jnp.zeros_like(counts_r_ref)
    counts_c_ref[...] = jnp.zeros_like(counts_c_ref)
    for h in range(hops):
        if h == hops - 1 and seqs > 1:
            hop(1, 0).start()
        advance(0, h)

    def sequence(s, carry):
        @pl.when(s + 2 < seqs)
        def _():
            hop(s + 2, 0).start()

        def follow(step):
            @pl.when(s + 1 < seqs)
            def _():
                for h in range(step * hops // STEPS, (step + 1) * hops // STEPS):
                    advance(s + 1, h)

        messages = (held.at[s], ping, pong)
        for step in range(STEPS):
            alpha = messages[step]
            last = step == STEPS - 1
            v_row = sum_k_ref[s, step : step + 1, :]

            def mix(i, total, alpha=alpha, last=last, step=step, v_row=v_row):
                at = pl.ds(pl.multiple_of(i * tile, tile), tile)
                block = alpha[at, :]
                mixed_own[at, :] = dot(block, cols_own_ref[...]).astype(BF16)
                if not last:
                    mixed[at, :] = dot(block, cols_ref[...]).astype(BF16)
                part = jnp.sum(block.astype(F32) * v_row, axis=1, keepdims=True)
                gain = sum_l_ref[s, at, step : step + 1]
                return total + jnp.sum(part * gain, axis=0, keepdims=True)

            total = lax.fori_loop(0, tiles, mix, jnp.zeros((1, 1), F32))
            norm = total / cells
            inv = 1.0 / norm
            norm_ref[s, step : step + 1, :] = jnp.broadcast_to(norm, (1, norm_ref.shape[2]))
            scaled_k = emit_k_own_ref[s, step : step + 1, :] * inv
            row_k = emit_k_ref[s, step : step + 1, :] * inv

            def weigh(i, carry, step=step, scaled_k=scaled_k):
                at = pl.ds(pl.multiple_of(i * tile, tile), tile)
                gain = emit_l_ref[s, at, step : step + 1]
                weight[at, :half] = (
                    back_mine_ref[step, s, at, :].astype(F32) * (gain * scaled_k[:, :half])
                ).astype(BF16)
                weight[at, half:] = (
                    back_other_ref[step, s, at, :].astype(F32) * (gain * scaled_k[:, half:])
                ).astype(BF16)
                return carry

            lax.fori_loop(0, tiles, weigh, 0)

            if not last:
                fresh = messages[step + 1]

                def move(i, carry, fresh=fresh, row_k=row_k, step=step):
                    at = pl.ds(pl.multiple_of(i * tile, tile), tile)
                    moved = dot(rows_t_ref[at, :], mixed[...])
                    gain = emit_l_ref[s, at, step : step + 1]
                    fresh[at, :] = (moved * (gain * row_k)).astype(BF16)
                    return carry

                lax.fori_loop(0, tiles, move, 0)
            else:
                rows_q = dot(rows_own_ref[...], alpha[...]).astype(BF16)
                moved = dot(rows_q, cols_ref[...])
                gain = emit_l_own_ref[s, :, step : step + 1]
                final_ref[s] = (moved * (gain * row_k)).astype(BF16)

            if not last:
                follow(step)

            def count(i, carry):
                at = pl.ds(pl.multiple_of(i * tile, tile), tile)
                pulled[at, :] = dot(rows_ref[at, :], weight[...]).astype(BF16)
                counts_r_ref[at, :] += dot(weight[at, :], mixed_own[...], NT)
                return carry

            lax.fori_loop(0, tiles, count, 0)
            counts_c_ref[...] += dot(pulled[...], alpha[...], TN)

            if last:
                follow(step)

        return carry

    lax.fori_loop(0, seqs, sequence, 0)
    for s in range(seqs):
        for h in range(hops):
            hop(s, h).wait_send()


def run_forward(chips, *operands):
    chip_rows, rows, _, cols, rows_own, cols_own = operands[:6]
    seqs = chip_rows.shape[0]
    width, cols_all = rows.shape[0], cols.shape[1]
    own_rows, own_cols = rows_own.shape[0], cols_own.shape[1]
    vmem = pl.BlockSpec(memory_space=pltpu.VMEM)
    flops = 2 * seqs * width * cols_all * (4 * width + 3 * 4 * own_cols + 2 * own_rows)
    message = pltpu.VMEM((width, cols_all), BF16)
    narrow = pltpu.VMEM((width, own_cols), BF16)
    return pl.pallas_call(
        functools.partial(forward_kernel, chips),
        out_shape=[
            jax.ShapeDtypeStruct((seqs, own_rows, cols_all), BF16),
            jax.ShapeDtypeStruct((width, width), F32),
            jax.ShapeDtypeStruct((own_cols, cols_all), F32),
            jax.ShapeDtypeStruct((seqs, STEPS, 128), F32),
        ],
        in_specs=[vmem] * len(operands),
        out_specs=[vmem] * 4,
        scratch_shapes=[
            pltpu.VMEM((seqs, width, cols_all), BF16),
            message,
            message,
            message,
            narrow,
            narrow,
            narrow,
            pltpu.SemaphoreType.DMA((seqs, chips - 1)),
            pltpu.SemaphoreType.DMA((seqs, chips - 1)),
        ],
        compiler_params=pltpu.CompilerParams(
            collective_id=0, has_side_effects=True, vmem_limit_bytes=58 * 1024 * 1024
        ),
        cost_estimate=pl.CostEstimate(
            flops=flops, bytes_accessed=40 * 1024 * 1024, transcendentals=0
        ),
    )(*operands)


def on_device(alpha_init, tokens, trans_rows, trans_cols, emit_rows, emit_cols, backward):
    groups = lax.axis_size("state")
    dp = lax.axis_size("dp")
    me = lax.axis_index("state")
    core = me % 2
    seq_dev, rows_dev, width_cols = alpha_init.shape
    width_rows = trans_rows.shape[0]
    cols_dev = width_cols // groups
    half = seq_dev // 2
    pairs = [(d, d ^ 1) for d in range(groups)]
    lines = [list(range(c, groups, 2)) for c in range(2)]

    def swap(x):
        return lax.ppermute(x, "state", pairs)

    def split(x, axis):
        mine = lax.dynamic_slice_in_dim(x, core * half, half, axis)
        return mine, lax.dynamic_slice_in_dim(x, (1 - core) * half, half, axis)

    alpha_mine, alpha_send = split(alpha_init, 0)
    alpha_other = swap(alpha_send)
    chip_rows = jnp.where(
        core == 0,
        jnp.concatenate([alpha_mine, alpha_other], 1),
        jnp.concatenate([alpha_other, alpha_mine], 1),
    )
    back_mine, back_send = split(backward, 1)
    back_other = swap(back_send)

    def own(x, size, axis):
        return jnp.concatenate(
            [
                lax.dynamic_slice_in_dim(x, me * size, size, axis),
                lax.dynamic_slice_in_dim(x, (me + 1 - 2 * core) * size, size, axis),
            ],
            axis,
        )

    rows_t = trans_rows.T
    shared = (trans_rows, rows_t, trans_cols, own(rows_t, rows_dev, 0), own(trans_cols, cols_dev, 1))
    tok = lax.dynamic_slice_in_dim(tokens, core * half, half, 0)
    first = jnp.take(emit_rows, tok, axis=0)
    second = jnp.take(emit_cols, tok, axis=0)
    sum_l = jnp.einsum("stl,il->sit", first, trans_rows, preferred_element_type=F32)
    sum_k = jnp.einsum("stk,jk->stj", second, trans_cols, preferred_element_type=F32)
    emit_l = jnp.swapaxes(first, 1, 2).astype(F32)
    emit_k = second.astype(F32)
    emit_l_own = own(emit_l, rows_dev, 1)
    emit_k_own = own(emit_k, cols_dev, 2)

    final, terms_r, terms_c, norms = run_forward(
        groups // 2,
        chip_rows,
        *shared,
        back_mine,
        back_other,
        emit_l,
        emit_k,
        emit_l_own,
        emit_k_own,
        sum_l,
        sum_k,
    )
    final_mine, final_other = final[:, :rows_dev], swap(final[:, rows_dev:])
    alpha_final = jnp.where(
        core == 0,
        jnp.concatenate([final_mine, final_other], 0),
        jnp.concatenate([final_other, final_mine], 0),
    )
    logs = jnp.sum(jnp.log(norms[:, :, 0]), axis=1)
    logs_other = swap(logs)
    loglik = jnp.where(
        core == 0, jnp.concatenate([logs, logs_other]), jnp.concatenate([logs_other, logs])
    )

    factor = 1.0 / (seq_dev * dp * STEPS)
    chips = groups // 2
    block = width_rows // (groups * dp)
    col_block = width_cols // (groups * dp)
    place = lax.axis_index("dp") * groups + me
    by_core = terms_r.reshape(dp, chips, 2, block, width_rows)

    def of_core(c, cols):
        rows = lax.dynamic_index_in_dim(by_core, c, 2, keepdims=False)
        return jnp.concatenate(
            [rows.reshape(dp, chips * block, width_rows), cols.reshape(dp, col_block, width_cols)], 1
        )

    here = of_core(core, terms_c[:cols_dev])
    there = swap(of_core(1 - core, terms_c[cols_dev:]).astype(BF16))
    both = (here + there.astype(F32)).astype(BF16)
    parts = lax.all_to_all(both, "dp", 0, 0, tiled=True)
    sums = jnp.sum(parts.astype(F32), axis=0)
    order = [(d * groups + g, g * dp + d) for d in range(dp) for g in range(groups)]
    sums_c = lax.ppermute(sums[chips * block :], ("dp", "state"), order)
    line = sums[: chips * block].reshape(chips, block, width_rows).astype(BF16)
    line = lax.all_to_all(line, "state", 0, 0, tiled=True, axis_index_groups=lines)
    sums_r = jnp.sum(line.astype(F32), axis=0)
    counts_rows = (
        lax.dynamic_slice_in_dim(rows_t, place * block, block, 0).astype(F32) * sums_r * factor
    ).T
    counts_cols = (
        lax.dynamic_slice_in_dim(trans_cols, place * col_block, col_block, 1).astype(F32)
        * sums_c.T
        * factor
    )
    return (alpha_final, counts_rows, counts_cols, loglik)


def solution(mesh):
    return jax.shard_map(
        on_device,
        mesh=mesh,
        in_specs=(
            P("dp", "state", None),
            P("dp", None),
            P(),
            P(),
            P(),
            P(),
            P(None, "dp", None, "state"),
        ),
        out_specs=(
            P("dp", "state", None),
            P(None, ("dp", "state")),
            P(None, ("dp", "state")),
            P("dp"),
        ),
        check_vma=False,
    )
```
